256 devices in a mesh: blk: 128 (over y, x_lo, z, core), rel: 2 (over x_hi).
Axes of the slice: x: 4 (x_hi: 2, x_lo: 2; x = x_hi * 2 + x_lo), y: 4, z: 8, core: 2. Of those that a mesh axis runs over, the one named last changes fastest.
Arguments:
- lhs_table: float32 [400, 32768], P(None, 'blk'), may hold values from -1.5 to 1.5
- rhs_table: float32 [400, 32768], P(None, 'blk'), may hold values from -1.5 to 1.5
- rel_table: float32 [400, 1280], P(None, 'rel'), may hold values from -2.4 to 2.4
- lhs_acc: float32 [32768], P('blk'), may hold values from 0.001 to 0.03
- rhs_acc: float32 [32768], P('blk'), may hold values from 0.001 to 0.03
- rel_acc: float32 [1280], P('rel'), may hold values from 0.003 to 3
- lhs_index: int32 [128, 2, 2, 1024], P('blk', 'rel'), may hold values from 0 to 255
- rhs_index: int32 [128, 2, 2, 1024], P('blk', 'rel'), may hold values from 0 to 255
- rel_index: int32 [128, 2, 2, 1024], P('blk', 'rel'), may hold values from 0 to 639
- bucket_ends: int32 [128, 2, 2], P('blk', 'rel'), may hold values from 1 to 1024, as said below
- neg_index: int32 [128, 2, 2, 4, 128], P('blk', 'rel'), may hold values from 0 to 255
Outputs:
- lhs_out: float32 [400, 32768], P(None, 'blk')
- lhs_acc_out: float32 [32768], P('blk')
- rhs_out: float32 [400, 32768], P(None, 'blk')
- rhs_acc_out: float32 [32768], P('blk')
- rel_out: float32 [400, 1280], P(None, 'rel')
- rel_acc_out: float32 [1280], P('rel')
The draws below stay inside these ranges and needn't reach their ends.
Inputs may be any that keep to these rules, and one draw needn't show every extreme that they name: Only the first bucket_ends slots of a bucket are live; every other slot, and every span without a live slot, is ignored. In every round at least one bucket is full.
All inputs are finite; a program needn't handle non-finite values.
Results may differ from the reference program's by a relative error of at most 0.0003.
Values sent between devices are 32-bit elements; how exact they have to be, the bound alone decides.
No kernel may reach another device: no remote copies, remote signals or barrier semaphores. Data moves between devices by JAX's collectives and lax.ppermute only.
A program may use at most 64 MiB of HBM per device.

```python
import math
import jax
import jax.numpy as jnp
import numpy as np
from jax import lax

D = 400
RELS = 1280
ROWS = 256
EDGE_CAP = 1024
NEG = 128
ROUNDS = 2
SPANS = 4
SLABS = 128
HALVES = 2
ENTITIES = 32768
N_REL = 2


def draw_bucket_ends(key, part):
    key = jax.random.fold_in(key, 11)
    first_key, second_key = jax.random.split(key)
    base = jax.random.randint(first_key, (SLABS * HALVES, ROUNDS), 0, EDGE_CAP)
    counts = 1 + base * base // EDGE_CAP
    fullest = jax.random.randint(second_key, (ROUNDS,), 0, SLABS * HALVES)
    picked = jnp.arange(SLABS * HALVES, dtype=jnp.int32)[:, None] == fullest[None, :]
    counts = jnp.where(picked, EDGE_CAP, counts)
    return counts.reshape(SLABS, HALVES, ROUNDS).astype(jnp.int32)


def plant(result, rng, low, top_value):
    shape = result.shape
    index_at = [jax.random.randint(jax.random.fold_in(rng, axis), (), 0, shape[axis]) for axis in range(len(shape))]
    result = result.at[tuple(index_at)].set(low)
    longest = shape.index(max(shape))
    index_at[longest] = (index_at[longest] + 1) % shape[longest]
    return result.at[tuple(index_at)].set(top_value)


def block_levels(key, shape, pieces, low, top_value):
    def one(axis_at, parts):
        steps = jax.random.uniform(jax.random.fold_in(jax.random.fold_in(key, 6), axis_at), (parts,), jnp.float32, low / len(pieces), top_value / len(pieces))
        return jnp.repeat(jnp.exp(steps), shape[axis_at] // parts).reshape((-1,) + (1,) * (len(shape) - axis_at - 1))

    gain = one(*pieces[0])
    for cut in pieces[1:]:
        gain = gain * one(*cut)
    return gain


def cumulative_ranks(number_of, slope):
    loads = [(1 << 20) // math.isqrt(rank ** slope) + 1 for rank in range(1, number_of + 1)]
    scale = 1 + sum(loads) // (1 << 30)
    return np.cumsum(np.array([max(1, weight // scale) for weight in loads]))


def skewed_ids(stream_key, extent, number_of, skew):
    table = cumulative_ranks(number_of, skew)
    ticket = jax.random.randint(jax.random.fold_in(stream_key, 1), extent, 0, int(table[number_of - 1]))
    standing = jnp.searchsorted(jnp.asarray(table, jnp.int32), ticket, side="right")
    return jax.random.permutation(jax.random.fold_in(stream_key, 2), number_of)[standing].astype(jnp.int32)


def gaussian(key, shape, scale, bound, shards=(), kind=jnp.bfloat16):
    entries = scale * jax.random.normal(key, shape, jnp.float32)
    if shards:
        entries = entries * block_levels(key, shape, shards, -0.22, 0.18)
    return jnp.clip(entries, -bound, bound).astype(kind)


def setup_inputs(seed: int = 0) -> dict:
    keys = jax.random.split(jax.random.key(seed), 12)
    return {
        "lhs_table": gaussian(keys[0], (D, ENTITIES), 0.25, 1.5, ((1, 128),), jnp.float32),
        "rhs_table": gaussian(keys[1], (D, ENTITIES), 0.25, 1.5, ((1, 128),), jnp.float32),
        "rel_table": gaussian(keys[2], (D, RELS), 0.4, 2.4, ((1, 2),), jnp.float32),
        "lhs_acc": jnp.clip(jnp.exp(math.log(0.03) - 3.4011973 * jax.random.uniform(keys[3], (ENTITIES,), jnp.float32) ** block_levels(keys[3], (ENTITIES,), ((0, 128),), -0.2, 0.2)), 0.001, 0.03),
        "rhs_acc": jnp.clip(jnp.exp(math.log(0.03) - 3.4011973 * jax.random.uniform(keys[4], (ENTITIES,), jnp.float32) ** block_levels(keys[4], (ENTITIES,), ((0, 128),), -0.2, 0.2)), 0.001, 0.03),
        "rel_acc": jnp.clip(jnp.exp(math.log(3.0) - 6.9077553 * jax.random.uniform(keys[5], (RELS,), jnp.float32) ** block_levels(keys[5], (RELS,), ((0, 2),), -0.2, 0.2)), 0.003, 3.0),
        "lhs_index": plant(jax.random.randint(keys[6], (SLABS, HALVES, ROUNDS, EDGE_CAP), 0, ROWS), jax.random.fold_in(keys[6], 1), 0, ROWS - 1).astype(jnp.int32),
        "rhs_index": plant(jax.random.randint(keys[7], (SLABS, HALVES, ROUNDS, EDGE_CAP), 0, ROWS), jax.random.fold_in(keys[7], 1), 0, ROWS - 1).astype(jnp.int32),
        "rel_index": plant(skewed_ids(keys[8], (SLABS, HALVES, ROUNDS, EDGE_CAP), RELS // N_REL, 2), jax.random.fold_in(keys[8], 3), 0, (RELS // N_REL) - 1).astype(jnp.int32),
        "bucket_ends": draw_bucket_ends(jax.random.fold_in(keys[11], 71), 0),
        "neg_index": plant(jax.random.randint(keys[10], (SLABS, HALVES, ROUNDS, SPANS, NEG), 0, ROWS), jax.random.fold_in(keys[10], 1), 0, ROWS - 1).astype(jnp.int32),
    }


STEP_SIZE = 0.2

def adagrad_rows(table, accumulator, gradient):
    grown = accumulator + lax.optimization_barrier(jnp.mean(gradient * gradient, axis=0))
    return (table - STEP_SIZE * gradient * lax.rsqrt(grown)[None, :], grown)

def bucket_gradients(lhs_slab, context_slab, relation_half, lhs_slots, rhs_slots, relation_slots, live_count, negative_slots):
    edge_count = lhs_slots.shape[0]
    span_count, negative_count = negative_slots.shape
    span_width = edge_count // span_count
    feature_count = lhs_slab.shape[0]
    live = (lax.iota(jnp.int32, edge_count) < live_count).astype(jnp.float32)
    left_rows = jnp.take(lhs_slab, lhs_slots, axis=1)
    right_rows = jnp.take(context_slab, rhs_slots, axis=1)
    weights = jnp.take(relation_half, relation_slots, axis=1)
    scaled = left_rows * weights
    positive = lax.optimization_barrier(jnp.sum(scaled * right_rows, axis=0))
    flat_negatives = negative_slots.reshape(-1)
    negative_rows = jnp.take(context_slab, flat_negatives, axis=1).reshape(feature_count, span_count, negative_count)
    scaled_blocks = scaled.reshape(feature_count, span_count, span_width)
    negative = jnp.einsum('dcw,dcn->cwn', scaled_blocks, negative_rows, precision=lax.Precision.HIGHEST)
    positive_coef = -jax.nn.sigmoid(-positive) * live
    negative_coef = jax.nn.sigmoid(negative) * (live.reshape(span_count, span_width, 1) / negative_count)
    mixture = jnp.einsum('cwn,dcn->dcw', negative_coef, negative_rows, precision=lax.Precision.HIGHEST).reshape(feature_count, edge_count)
    toward = positive_coef[None, :] * right_rows + mixture
    negative_grad = jnp.einsum('cwn,dcw->dcn', negative_coef, scaled_blocks, precision=lax.Precision.HIGHEST).reshape(feature_count, span_count * negative_count)
    lhs_grad = jnp.zeros_like(lhs_slab).at[:, lhs_slots].add(weights * toward)
    context_grad = jnp.zeros_like(context_slab).at[:, rhs_slots].add(positive_coef[None, :] * scaled)
    context_grad = context_grad.at[:, flat_negatives].add(negative_grad)
    relation_grad = jnp.zeros_like(relation_half).at[:, relation_slots].add(left_rows * toward)
    return (lhs_grad, context_grad, relation_grad)

def reference(lhs_table, rhs_table, rel_table, lhs_acc, rhs_acc, rel_acc, lhs_index, rhs_index, rel_index, bucket_ends, neg_index):
    part_count = lhs_index.shape[0]
    half_count = lhs_index.shape[1]
    round_count = lhs_index.shape[2]
    feature_count = lhs_table.shape[0]
    slab_rows = lhs_table.shape[1] // part_count
    half_rels = rel_table.shape[1] // half_count
    for t in range(round_count):

        def one_block(carry, b):
            lhs_slab = lax.dynamic_slice_in_dim(lhs_table, b * slab_rows, slab_rows, 1)
            context = ((b - t) % part_count).astype(jnp.int32)
            context_slab = lax.dynamic_slice_in_dim(rhs_table, context * slab_rows, slab_rows, 1)
            lhs_total = jnp.zeros_like(lhs_slab)
            context_total = jnp.zeros_like(context_slab)
            relation_parts = []
            for k in range(half_count):
                relation_half = rel_table[:, k * half_rels:(k + 1) * half_rels]
                lhs_grad, context_grad, relation_grad = bucket_gradients(lhs_slab, context_slab, relation_half, lhs_index[b, k, t], rhs_index[b, k, t], rel_index[b, k, t], bucket_ends[b, k, t], neg_index[b, k, t])
                lhs_total = lhs_total + lhs_grad
                context_total = context_total + context_grad
                relation_parts.append(relation_grad)
            return (carry + jnp.concatenate(relation_parts, axis=1), (lhs_total, context_total))
        relation_sum, stacked = lax.scan(one_block, jnp.zeros_like(rel_table), jnp.arange(part_count, dtype=jnp.int32))
        lhs_stack, context_stack = stacked
        lhs_grad_all = lhs_stack.transpose(1, 0, 2).reshape(feature_count, part_count * slab_rows)
        context_stack = jnp.roll(context_stack, -t, axis=0)
        rhs_grad_all = context_stack.transpose(1, 0, 2).reshape(feature_count, part_count * slab_rows)
        lhs_table, lhs_acc = adagrad_rows(lhs_table, lhs_acc, lhs_grad_all)
        rhs_table, rhs_acc = adagrad_rows(rhs_table, rhs_acc, rhs_grad_all)
        rel_table, rel_acc = adagrad_rows(rel_table, rel_acc, relation_sum)
    rhs_out = jnp.roll(rhs_table.reshape(feature_count, part_count, slab_rows), round_count - 1, axis=1).reshape(feature_count, part_count * slab_rows)
    rhs_acc_out = jnp.roll(rhs_acc.reshape(part_count, slab_rows), round_count - 1, axis=0).reshape(part_count * slab_rows)
    return (lhs_table, lhs_acc, rhs_out, rhs_acc_out, rel_table, rel_acc)
```

```python
import functools

import jax
import jax.numpy as jnp
from jax import lax
from jax.experimental import pallas as pl
from jax.experimental.pallas import tpu as pltpu
from jax.sharding import PartitionSpec as P

STEP_SIZE = 0.2
F32 = jnp.float32
BF16 = jnp.bfloat16
LANES = 128
VMEM_LIMIT = 48 * 1024 * 1024


def split(x):
    hi = x.astype(BF16)
    return hi, (x - hi.astype(F32)).astype(BF16)


def nn(a, b):
    return jnp.dot(a, b, preferred_element_type=F32)


def nt(a, b):
    return lax.dot_general(a, b, (((1,), (1,)), ((), ())), preferred_element_type=F32)


def one_hot(row, count):
    ids = lax.broadcasted_iota(jnp.int32, (count, row.shape[1]), 0)
    return jnp.where(ids == row, 1.0, 0.0).astype(BF16)


def adagrad(table, acc, grad):
    grown = acc + jnp.sum(grad * grad, axis=0, keepdims=True) * (1.0 / grad.shape[0])
    return table - STEP_SIZE * grad * lax.rsqrt(grown), grown


def gradients(t, refs, lhs_ref, rhs_ref, rel_ref, outs):
    (lidx, ridx, widx, nidx, ends) = refs
    (glhs_ref, gctx_ref, grel_ref) = outs
    d, rows = lhs_ref.shape
    rels = rel_ref.shape[1]
    edges = lidx.shape[1]
    neg = nidx.shape[1]
    spans = nidx.shape[0] // lidx.shape[0]
    width = edges // spans
    live_count = ends[t]
    lhi, llo = split(lhs_ref[...])
    rhi, rlo = split(rhs_ref[...])
    whi, wlo = split(rel_ref[...])
    for c in range(spans):
        at = pl.ds(c * width, width)
        hot_l = one_hot(lidx[pl.ds(t, 1), at], rows)
        hot_r = one_hot(ridx[pl.ds(t, 1), at], rows)
        hot_w = one_hot(widx[pl.ds(t, 1), at], rels)
        hot_n = one_hot(nidx[pl.ds(t * spans + c, 1), :], rows)
        left = nn(lhi, hot_l) + nn(llo, hot_l)
        right = nn(rhi, hot_r) + nn(rlo, hot_r)
        weights = nn(whi, hot_w) + nn(wlo, hot_w)
        qh32 = nn(rhi, hot_n)
        ql32 = nn(rlo, hot_n)
        qh, ql = qh32.astype(BF16), ql32.astype(BF16)
        qht, qlt = qh32.T.astype(BF16), ql32.T.astype(BF16)
        scaled = left * weights
        sh, sl = split(scaled)
        scores = nn(qht, sh) + (nn(qht, sl) + nn(qlt, sh))
        slot = lax.broadcasted_iota(jnp.int32, (1, width), 1) + c * width
        live = jnp.where(slot < live_count, 1.0, 0.0)
        coef = jax.nn.sigmoid(scores) * (live / neg)
        positive = jnp.sum(scaled * right, axis=0, keepdims=True)
        pcoef = -jax.nn.sigmoid(-positive) * live
        ch, cl = split(coef)
        toward = pcoef * right + (nn(qh, ch) + (nn(qh, cl) + nn(ql, ch)))
        ngh, ngl = split(nt(sh, ch) + (nt(sh, cl) + nt(sl, ch)))
        uh, ul = split(left * toward)
        grel = nt(uh, hot_w) + nt(ul, hot_w)
        vh, vl = split(weights * toward)
        glhs = nt(vh, hot_l) + nt(vl, hot_l)
        ph, pw = split(pcoef * scaled)
        gctx = nt(ph, hot_r) + nt(pw, hot_r) + nt(ngh, hot_n) + nt(ngl, hot_n)
        for b in range(rels // LANES):
            part = grel[:, b * LANES:(b + 1) * LANES]
            if c == 0:
                grel_ref[pl.ds(b * d, d), :] = part
            else:
                grel_ref[pl.ds(b * d, d), :] += part
        if c == 0:
            glhs_ref[...] = glhs
            gctx_ref[...] = gctx
        else:
            glhs_ref[...] += glhs
            gctx_ref[...] += gctx


def halves(core, grel_ref, keep_ref, send_ref, used):
    half = keep_ref.shape[0]
    grel_ref[pl.ds(used, grel_ref.shape[0] - used), :] = jnp.zeros(
        (grel_ref.shape[0] - used, LANES), F32
    )
    keep_ref[...] = grel_ref[pl.ds(pl.multiple_of(core * half, half), half), :]
    send_ref[...] = grel_ref[pl.ds(pl.multiple_of((1 - core) * half, half), half), :]


def first_kernel(lidx, ridx, widx, nidx, ends, core, lhs, rhs, rel,
                 glhs, gctx, keep, send, grel):
    gradients(0, (lidx, ridx, widx, nidx, ends), lhs, rhs, rel, (glhs, gctx, grel))
    halves(core[0], grel, keep, send, rel.shape[0] * (rel.shape[1] // LANES))


def join(core, mine, other, grel):
    half = mine.shape[0]
    grel[pl.ds(pl.multiple_of(core * half, half), half), :] = mine[...]
    grel[pl.ds(pl.multiple_of((1 - core) * half, half), half), :] = other[...]


def update_rel(rel, racc, grel, rel_new, racc_new):
    d = rel.shape[0]
    for b in range(rel.shape[1] // LANES):
        at = pl.ds(b * LANES, LANES)
        g = grel[pl.ds(b * d, d), :]
        rel_new[:, at], racc_new[:, at] = adagrad(rel[:, at], racc[:, at], g)


def update_pair(table, acc, one, two, table_new, acc_new):
    table_new[...], acc_new[...] = adagrad(table[...], acc[...], one[...] + two[...])


def second_kernel(lidx, ridx, widx, nidx, ends, core, lhs, rhs, rel, lacc, racc, wacc,
                  gl_a, gl_b, gc_a, gc_b, gw_mine, gw_other,
                  glhs, gctx, keep, send, lhs_new, rhs_new, rel_new,
                  lacc_new, racc_new, wacc_new, grel):
    update_pair(lhs, lacc, gl_a, gl_b, lhs_new, lacc_new)
    update_pair(rhs, racc, gc_a, gc_b, rhs_new, racc_new)
    join(core[0], gw_mine, gw_other, grel)
    update_rel(rel, wacc, grel, rel_new, wacc_new)
    gradients(1, (lidx, ridx, widx, nidx, ends), lhs_new, rhs_new, rel_new, (glhs, gctx, grel))
    halves(core[0], grel, keep, send, rel.shape[0] * (rel.shape[1] // LANES))


def pair_kernel(lhs, rhs, lacc, racc, gl_a, gl_b, gc_a, gc_b, lhs_new, rhs_new, lacc_new, racc_new):
    update_pair(lhs, lacc, gl_a, gl_b, lhs_new, lacc_new)
    update_pair(rhs, racc, gc_a, gc_b, rhs_new, racc_new)


def rel_kernel(core, rel, wacc, gw_mine, gw_other, rel_new, wacc_new, grel):
    join(core[0], gw_mine, gw_other, grel)
    update_rel(rel, wacc, grel, rel_new, wacc_new)


VM = pl.BlockSpec(memory_space=pltpu.VMEM)
SM = pl.BlockSpec(memory_space=pltpu.SMEM)


def call(kernel, ins, smem_at, outs, scratch, flops):
    return pl.pallas_call(
        kernel,
        out_shape=[jax.ShapeDtypeStruct(s, F32) for s in outs],
        in_specs=[SM if i in smem_at else VM for i in range(len(ins))],
        out_specs=[VM] * len(outs),
        scratch_shapes=[pltpu.VMEM(s, F32) for s in scratch],
        compiler_params=pltpu.CompilerParams(vmem_limit_bytes=VMEM_LIMIT),
        cost_estimate=pl.CostEstimate(
            flops=flops, bytes_accessed=8_000_000, transcendentals=0
        ),
    )(*ins)


def place(y, x, z, core):
    return y * 32 + x * 16 + z * 2 + core


def chip_chunk(y, x, z):
    return ((((y ^ (y >> 1)) & 1) * 2 + x) * 2) + ((z ^ (z >> 1)) & 1)


def cube_groups():
    groups = []
    for core in range(2):
        for yh in range(2):
            for zh in range(4):
                members = [None] * 8
                for yl in range(2):
                    for x in range(2):
                        for zl in range(2):
                            y, z = yh * 2 + yl, zh * 2 + zl
                            members[chip_chunk(y, x, z)] = place(y, x, z, core)
                groups.append(members)
    return groups


def pairs(move):
    out = []
    for y in range(4):
        for x in range(2):
            for z in range(8):
                for core in range(2):
                    a = place(y, x, z, core)
                    out.append((a, place(*move(y, x, z, core))))
    return out


CORE_PAIRS = pairs(lambda y, x, z, c: (y, x, z, 1 - c))
FAR_PAIRS = (
    pairs(lambda y, x, z, c: (3 - y, x, z, c)),
    pairs(lambda y, x, z, c: (y, x, (z + (1 if z % 2 else 7)) % 8, c)),
    pairs(lambda y, x, z, c: (y, x, z ^ (3 if z in (0, 3, 4, 7) else 7), c)),
)


def sum_over_blk(keep, send):
    part = keep + lax.ppermute(send, "blk", CORE_PAIRS)
    rows = part.shape[0] // 8
    groups = cube_groups()
    got = lax.all_to_all(
        part.reshape(8, rows, LANES), "blk", 0, 0, axis_index_groups=groups
    )
    total = jnp.sum(got, axis=0)
    for move in FAR_PAIRS:
        total = total + lax.ppermute(total, "blk", move)
    spread = jnp.broadcast_to(total[None], (8, rows, LANES))
    mine = lax.all_to_all(spread, "blk", 0, 0, axis_index_groups=groups)
    mine = mine.reshape(8 * rows, LANES)
    return mine, lax.ppermute(mine, "blk", CORE_PAIRS)


def swap(x):
    return lax.ppermute(x, "rel", [(0, 1), (1, 0)])


def onward(x, flip):
    n = lax.axis_size("blk")
    moves = [
        (2 * b + k, 2 * ((b + 1) % n) + (1 - k if flip else k)) for b in range(n) for k in range(2)
    ]
    return lax.ppermute(x, ("blk", "rel"), moves)


def per_device(lhs, rhs, rel, lacc, racc, wacc, lidx, ridx, widx, ends, nidx):
    d, rows = lhs.shape
    rels = rel.shape[1]
    rounds, edges = lidx.shape[2:]
    spans, neg = nidx.shape[3:]
    lidx, ridx, widx = (a.reshape(rounds, edges) for a in (lidx, ridx, widx))
    nidx = nidx.reshape(rounds * spans, neg)
    ends = ends.reshape(rounds)
    lacc, racc, wacc = (a.reshape(1, -1) for a in (lacc, racc, wacc))
    core = lax.rem(lax.axis_index("blk"), 2).astype(jnp.int32).reshape(1)
    used = d * (rels // LANES)
    full = -(-used // 2048) * 2048
    slab, table, state = (d, rows), (d, rels), (1, rows)
    half = (full // 2, LANES)
    index = (lidx, ridx, widx, nidx, ends, core)

    rhs_next = onward(rhs, False)
    racc_next = onward(racc, False)
    glhs, gctx, keep, send = call(
        first_kernel, index + (lhs, rhs, rel), (4, 5), [slab, slab, half, half],
        [(full, LANES)], 4_000_000_000,
    )
    gw_mine, gw_other = sum_over_blk(keep, send)
    gl_other = swap(glhs)
    gc_a = onward(gctx, False)
    gc_b = onward(gctx, True)
    glhs, gctx, keep, send, lhs, rhs, rel, lacc, racc, wacc = call(
        second_kernel,
        index + (lhs, rhs_next, rel, lacc, racc_next, wacc,
                 glhs, gl_other, gc_a, gc_b, gw_mine, gw_other),
        (4, 5),
        [slab, slab, half, half, slab, slab, table, state, state, (1, rels)],
        [(full, LANES)], 4_000_000_000,
    )
    gw_mine, gw_other = sum_over_blk(keep, send)
    gl_other = swap(glhs)
    gc_other = swap(gctx)
    lhs, rhs, lacc, racc = call(
        pair_kernel, (lhs, rhs, lacc, racc, glhs, gl_other, gctx, gc_other), (),
        [slab, slab, state, state], [], 1_000_000,
    )
    rel, wacc = call(
        rel_kernel, (core, rel, wacc, gw_mine, gw_other), (0,), [table, (1, rels)],
        [(full, LANES)], 1_000_000,
    )
    return lhs, lacc.reshape(-1), rhs, racc.reshape(-1), rel, wacc.reshape(-1)


def solution(mesh):
    in_specs = (
        P(None, "blk"),
        P(None, "blk"),
        P(None, "rel"),
        P("blk"),
        P("blk"),
        P("rel"),
        P("blk", "rel", None, None),
        P("blk", "rel", None, None),
        P("blk", "rel", None, None),
        P("blk", "rel", None),
        P("blk", "rel", None, None, None),
    )
    out_specs = (P(None, "blk"), P("blk"), P(None, "blk"), P("blk"), P(None, "rel"), P("rel"))
    return jax.shard_map(
        per_device, mesh=mesh, in_specs=in_specs, out_specs=out_specs, check_vma=False
    )
```

```python
import functools

import jax
import jax.numpy as jnp
from jax import lax
from jax.experimental import pallas as pl
from jax.experimental.pallas import tpu as pltpu
from jax.sharding import PartitionSpec as P

STEP_SIZE = 0.2
F32 = jnp.float32
BF16 = jnp.bfloat16
LANES = 128


def split(x):
    hi = x.astype(BF16)
    return hi, (x - hi.astype(F32)).astype(BF16)


def nn(a, b):
    return jnp.dot(a, b, preferred_element_type=F32)


def nt(a, b):
    return lax.dot_general(a, b, (((1,), (1,)), ((), ())), preferred_element_type=F32)


def one_hot(row, count):
    ids = lax.broadcasted_iota(jnp.int32, (count, row.shape[1]), 0)
    return jnp.where(ids == row, 1.0, 0.0).astype(BF16)


def adagrad(table, acc, grad):
    grown = acc + jnp.sum(grad * grad, axis=0, keepdims=True) * (1.0 / grad.shape[0])
    return table - STEP_SIZE * grad * lax.rsqrt(grown), grown


def bucket(t, spans, idx, ends, tables, outs, work):
    (lidx, ridx, widx, nidx) = idx
    (lhs, rhs, rel) = tables
    (glhs, gctx, grel) = outs
    (left, right, wts, hot_w, qh, ql, qht, qlt, sh, sl, uh, ul, vh, vl, ph, pw, nh, nl) = work
    d, rows = lhs.shape
    rels = rel.shape[1]
    edges = lidx.shape[1]
    neg = nidx.shape[1]
    width = edges // spans
    ats = [pl.ds(c * width, width) for c in range(spans)]
    nats = [pl.ds(c * neg, neg) for c in range(spans)]

    def hot_neg(c):
        return one_hot(nidx[pl.ds(t * spans + c, 1), :], rows)

    rh, rl = split(rhs[...])
    for c in range(spans):
        hot_n = hot_neg(c)
        q = nn(rh, hot_n)
        qh[:, nats[c]] = q.astype(BF16)
        qht[nats[c], :] = q.T.astype(BF16)
        q = nn(rl, hot_n)
        ql[:, nats[c]] = q.astype(BF16)
        qlt[nats[c], :] = q.T.astype(BF16)
    for c in range(spans):
        hot = one_hot(ridx[pl.ds(t, 1), ats[c]], rows)
        right[:, ats[c]] = nn(rh, hot) + nn(rl, hot)
    rh, rl = split(lhs[...])
    for c in range(spans):
        hot = one_hot(lidx[pl.ds(t, 1), ats[c]], rows)
        left[:, ats[c]] = nn(rh, hot) + nn(rl, hot)
    rh, rl = split(rel[...])
    pcoefs, lives = [], []
    for c in range(spans):
        hot = one_hot(widx[pl.ds(t, 1), ats[c]], rels)
        hot_w[:, ats[c]] = hot
        weights = nn(rh, hot) + nn(rl, hot)
        wts[:, ats[c]] = weights
        scaled = left[:, ats[c]] * weights
        high, low = split(scaled)
        sh[:, ats[c]] = high
        sl[:, ats[c]] = low
        slot = lax.broadcasted_iota(jnp.int32, (1, width), 1) + c * width
        live = jnp.where(slot < ends[t], 1.0, 0.0)
        positive = jnp.sum(scaled * right[:, ats[c]], axis=0, keepdims=True)
        pcoef = -jax.nn.sigmoid(-positive) * live
        ph[:, ats[c]], pw[:, ats[c]] = split(pcoef * scaled)
        pcoefs.append(pcoef)
        lives.append(live)
    coefs = []
    for c in range(spans):
        scores = nn(qht[nats[c], :], sh[:, ats[c]]) + (
            nn(qht[nats[c], :], sl[:, ats[c]]) + nn(qlt[nats[c], :], sh[:, ats[c]])
        )
        coefs.append(split(jax.nn.sigmoid(scores) * (lives[c] / neg)))
    for c in range(spans):
        ch, cl = coefs[c]
        mixture = nn(qh[:, nats[c]], ch) + (nn(qh[:, nats[c]], cl) + nn(ql[:, nats[c]], ch))
        toward = pcoefs[c] * right[:, ats[c]] + mixture
        uh[:, ats[c]], ul[:, ats[c]] = split(left[:, ats[c]] * toward)
        vh[:, ats[c]], vl[:, ats[c]] = split(wts[:, ats[c]] * toward)
    for c in range(spans):
        ch, cl = coefs[c]
        ngrad = nt(sh[:, ats[c]], ch) + (nt(sh[:, ats[c]], cl) + nt(sl[:, ats[c]], ch))
        nh[:, nats[c]], nl[:, nats[c]] = split(ngrad)
    total = nt(uh[...], hot_w[...]) + nt(ul[...], hot_w[...])
    for b in range(rels // LANES):
        grel[pl.ds(b * d, d), :] = total[:, b * LANES:(b + 1) * LANES]
    hot = one_hot(lidx[pl.ds(t, 1), :], rows)
    glhs[...] = nt(vh[...], hot) + nt(vl[...], hot)
    hot = one_hot(ridx[pl.ds(t, 1), :], rows)
    total = nt(ph[...], hot) + nt(pw[...], hot)
    hot = jnp.concatenate([hot_neg(c) for c in range(spans)], axis=1)
    gctx[...] = total + (nt(nh[...], hot) + nt(nl[...], hot))


def work_shapes(d, edges, negs, rels):
    f32 = [pltpu.VMEM((d, edges), F32)] * 3
    bf = lambda *shape: pltpu.VMEM(shape, BF16)
    return f32 + [bf(rels, edges)] + [bf(d, negs)] * 2 + [bf(negs, d)] * 2 + [bf(d, edges)] * 8 + [
        bf(d, negs)
    ] * 2


def halves(core, grel_ref, keep_ref, send_ref, used):
    half = keep_ref.shape[0]
    grel_ref[pl.ds(used, grel_ref.shape[0] - used), :] = jnp.zeros(
        (grel_ref.shape[0] - used, LANES), F32
    )
    keep_ref[...] = grel_ref[pl.ds(pl.multiple_of(core * half, half), half), :]
    send_ref[...] = grel_ref[pl.ds(pl.multiple_of((1 - core) * half, half), half), :]


def first_kernel(spans, core, lidx_hbm, ridx_hbm, nidx_hbm, widx_hbm, ends_hbm, rhs_hbm, lhs_hbm,
                 rel_hbm, glhs, gctx, keep, send, grel,
                 lidx, ridx, nidx, widx, ends, rhs, lhs, rel, sems, *work):
    sources = (lidx_hbm, ridx_hbm, nidx_hbm, widx_hbm, ends_hbm, rhs_hbm, lhs_hbm, rel_hbm)
    targets = (lidx, ridx, nidx, widx, ends, rhs, lhs, rel)
    copies = [
        pltpu.make_async_copy(source, target, sems.at[i])
        for i, (source, target) in enumerate(zip(sources, targets))
    ]
    for copy in copies:
        copy.start()
    for copy in copies:
        copy.wait()
    bucket(0, spans, (lidx, ridx, widx, nidx), ends, (lhs, rhs, rel), (glhs, gctx, grel), work)
    halves(core[0], grel, keep, send, rel.shape[0] * (rel.shape[1] // LANES))


def join(core, mine, other, grel):
    half = mine.shape[0]
    grel[pl.ds(pl.multiple_of(core * half, half), half), :] = mine[...]
    grel[pl.ds(pl.multiple_of((1 - core) * half, half), half), :] = other[...]


def update_rel(rel, racc, grel, rel_new, racc_new):
    d = rel.shape[0]
    for b in range(rel.shape[1] // LANES):
        at = pl.ds(b * LANES, LANES)
        g = grel[pl.ds(b * d, d), :]
        rel_new[:, at], racc_new[:, at] = adagrad(rel[:, at], racc[:, at], g)


def update_pair(table, acc, one, two, table_new, acc_new):
    table_new[...], acc_new[...] = adagrad(table[...], acc[...], one[...] + two[...])


def second_kernel(spans, lidx, ridx, widx, nidx, ends, core, lhs, rhs, rel, wacc,
                  gw_mine, gw_other, glhs, gctx, keep, send, rel_out, wacc_new,
                  grel, rel_new, sem, *work):
    join(core[0], gw_mine, gw_other, grel)
    update_rel(rel, wacc, grel, rel_new, wacc_new)
    copy = pltpu.make_async_copy(rel_new, rel_out, sem)
    copy.start()
    bucket(1, spans, (lidx, ridx, widx, nidx), ends, (lhs, rhs, rel_new), (glhs, gctx, grel), work)
    halves(core[0], grel, keep, send, rel.shape[0] * (rel.shape[1] // LANES))
    copy.wait()


def pair_kernel(lhs, rhs, lacc, racc, gl_a, gl_b, gc_a, gc_b, lhs_new, rhs_new, lacc_new, racc_new):
    update_pair(lhs, lacc, gl_a, gl_b, lhs_new, lacc_new)
    update_pair(rhs, racc, gc_a, gc_b, rhs_new, racc_new)


def rel_kernel(core, rel, wacc, gw_mine, gw_other, rel_new, wacc_new, grel):
    join(core[0], gw_mine, gw_other, grel)
    update_rel(rel, wacc, grel, rel_new, wacc_new)


def add_kernel(one, two, out):
    out[...] = one[...] + two[...]


def spread_kernel(one, two, *rest):
    out = rest[-1]
    out[...] = jnp.broadcast_to((one[...] + two[...])[None], out.shape)


def follow(value, others):
    return pl.pallas_call(
        lambda *refs: None,
        out_shape=jax.ShapeDtypeStruct(value.shape, value.dtype),
        in_specs=[AN] * (1 + len(others)),
        out_specs=AN,
        input_output_aliases={0: 0},
        compiler_params=pltpu.CompilerParams(vmem_limit_bytes=1 << 20),
    )(value, *others)


VM = pl.BlockSpec(memory_space=pltpu.VMEM)
SM = pl.BlockSpec(memory_space=pltpu.SMEM)
HB = pl.BlockSpec(memory_space=pltpu.HBM)
AN = pl.BlockSpec(memory_space=pl.ANY)


def call(kernel, ins, specs, outs, scratch, flops, mib=4, out_specs={}):
    return pl.pallas_call(
        kernel,
        out_shape=[jax.ShapeDtypeStruct(o, F32) if isinstance(o, tuple) else o for o in outs],
        in_specs=[specs.get(i, VM) for i in range(len(ins))],
        out_specs=[out_specs.get(i, VM) for i in range(len(outs))],
        scratch_shapes=[pltpu.VMEM(s, F32) if isinstance(s, tuple) else s for s in scratch],
        compiler_params=pltpu.CompilerParams(vmem_limit_bytes=mib << 20),
        cost_estimate=pl.CostEstimate(
            flops=flops, bytes_accessed=8_000_000, transcendentals=0
        ),
    )(*ins)


def place(y, x, z, core):
    return y * 32 + x * 16 + z * 2 + core


def near_groups():
    groups = []
    for core in range(2):
        for zh in range(4):
            members = [None] * 16
            for y in range(4):
                for x in range(2):
                    for zl in range(2):
                        z = zh * 2 + zl
                        members[(y * 2 + x) * 2 + ((z ^ (z >> 1)) & 1)] = place(y, x, z, core)
            groups.append(members)
    return groups


def pairs(move):
    out = []
    for y in range(4):
        for x in range(2):
            for z in range(8):
                for core in range(2):
                    a = place(y, x, z, core)
                    out.append((a, place(*move(y, x, z, core))))
    return out


CORE_PAIRS = pairs(lambda y, x, z, c: (y, x, z, 1 - c))
FAR_PAIRS = (
    pairs(lambda y, x, z, c: (y, x, (z + (1 if z % 2 else 7)) % 8, c)),
    pairs(lambda y, x, z, c: (y, x, z ^ (3 if z in (0, 3, 4, 7) else 7), c)),
)


def sum_over_blk(keep, send, exchange, after, wait_for):
    got = lax.ppermute(send, "blk", CORE_PAIRS)
    half = keep.shape
    (part,) = call(add_kernel, (keep, got), {}, [half], [], 1_000_000)
    beside = exchange()
    groups = near_groups()
    n = len(groups[0])
    rows = half[0] // n
    got = lax.all_to_all(
        part.reshape(n, rows, LANES), "blk", 0, 0, axis_index_groups=groups
    )
    total = jnp.sum(got, axis=0)
    total = total + lax.ppermute(total, "blk", FAR_PAIRS[0])
    got = lax.ppermute(total, "blk", FAR_PAIRS[1])
    ended = tuple(beside[1:])
    (spread,) = call(
        spread_kernel, (total, got) + ended, {2 + i: AN for i in range(len(ended))},
        [(n, rows, LANES)], [], 1_000_000,
    )
    mine = lax.all_to_all(spread, "blk", 0, 0, axis_index_groups=groups)
    beside = after(beside)
    mine = mine.reshape(n * rows, LANES)
    if wait_for:
        mine = follow(mine, tuple(beside[:1]))
    return mine, lax.ppermute(mine, "blk", CORE_PAIRS), beside


def swap(x):
    return lax.ppermute(x, "rel", [(0, 1), (1, 0)])


def onward(x, flip):
    n = lax.axis_size("blk")
    moves = [
        (2 * b + k, 2 * ((b + 1) % n) + (1 - k if flip else k)) for b in range(n) for k in range(2)
    ]
    return lax.ppermute(x, ("blk", "rel"), moves)


def per_device(lhs, rhs, rel, lacc, racc, wacc, lidx, ridx, widx, ends, nidx):
    d, rows = lhs.shape
    rels = rel.shape[1]
    rounds, edges = lidx.shape[2:]
    spans, neg = nidx.shape[3:]
    lidx, ridx, widx = (a.reshape(rounds, edges) for a in (lidx, ridx, widx))
    nidx = nidx.reshape(rounds * spans, neg)
    ends = ends.reshape(rounds)
    lacc, racc, wacc = (a.reshape(1, -1) for a in (lacc, racc, wacc))
    core = lax.rem(lax.axis_index("blk"), 2).astype(jnp.int32).reshape(1)
    used = d * (rels // LANES)
    full = -(-used // 2048) * 2048
    slab, table, state = (d, rows), (d, rels), (1, rows)
    half = (full // 2, LANES)
    work = work_shapes(d, edges, spans * neg, rels)
    sources = tuple(
        pltpu.with_memory_space_constraint(a, pltpu.HBM)
        for a in (lidx, ridx, nidx, widx, ends, rhs, lhs, rel)
    )
    glhs, gctx, keep, send = call(
        functools.partial(first_kernel, spans), (core,) + sources,
        {0: SM} | {1 + i: HB for i in range(8)},
        [slab, slab, half, half],
        [(full, LANES)]
        + [pltpu.VMEM(a.shape, a.dtype) for a in (lidx, ridx, nidx, widx)]
        + [pltpu.SMEM(ends.shape, ends.dtype), slab, slab, table, pltpu.SemaphoreType.DMA((8,))]
        + work,
        4_000_000_000, 40,
    )

    def exchange_first():
        return (glhs, swap(glhs), onward(gctx, False), onward(gctx, True),
                onward(rhs, False), onward(racc, False))

    def update_first(arrived):
        gl_a, gl_b, gc_a, gc_b, rhs_in, racc_in = arrived
        return call(
            pair_kernel, (lhs, rhs_in, lacc, racc_in, gl_a, gl_b, gc_a, gc_b), {},
            [slab, slab, state, state], [], 1_000_000, 2,
        )

    gw_mine, gw_other, (lhs1, rhs1, lacc1, racc1) = sum_over_blk(
        keep, send, exchange_first, update_first, True
    )
    glhs1, gctx1, keep, send, rel, wacc = call(
        functools.partial(second_kernel, spans),
        (lidx, ridx, widx, nidx, ends, core, lhs1, rhs1, rel, wacc, gw_mine, gw_other),
        {4: SM, 5: SM},
        [slab, slab, half, half, pltpu.HBM(table, F32), (1, rels)],
        [(full, LANES), table, pltpu.SemaphoreType.DMA] + work, 4_000_000_000, 40, {4: HB},
    )

    def exchange_last():
        return glhs1, swap(glhs1), gctx1, swap(gctx1)

    def update_last(arrived):
        return call(
            pair_kernel, (lhs1, rhs1, lacc1, racc1) + tuple(arrived), {},
            [slab, slab, state, state], [], 1_000_000, 2,
        )

    gw_mine, gw_other, (lhs, rhs, lacc, racc) = sum_over_blk(
        keep, send, exchange_last, update_last, False
    )
    rel, wacc = call(
        rel_kernel, (core, rel, wacc, gw_mine, gw_other), {0: SM}, [table, (1, rels)],
        [(full, LANES)], 1_000_000, 4,
    )
    return lhs, lacc.reshape(-1), rhs, racc.reshape(-1), rel, wacc.reshape(-1)


def solution(mesh):
    in_specs = (
        P(None, "blk"),
        P(None, "blk"),
        P(None, "rel"),
        P("blk"),
        P("blk"),
        P("rel"),
        P("blk", "rel", None, None),
        P("blk", "rel", None, None),
        P("blk", "rel", None, None),
        P("blk", "rel", None),
        P("blk", "rel", None, None, None),
    )
    out_specs = (P(None, "blk"), P("blk"), P(None, "blk"), P("blk"), P(None, "rel"), P("rel"))
    return jax.shard_map(
        per_device, mesh=mesh, in_specs=in_specs, out_specs=out_specs, check_vma=False
    )
```

```python
import functools

import jax
import jax.numpy as jnp
from jax import lax
from jax.experimental import pallas as pl
from jax.experimental.pallas import tpu as pltpu
from jax.sharding import PartitionSpec as P

STEP_SIZE = 0.2
F32 = jnp.float32
BF16 = jnp.bfloat16
LANES = 128


def split(x):
    hi = x.astype(BF16)
    return hi, (x - hi.astype(F32)).astype(BF16)


def nn(a, b):
    return jnp.dot(a, b, preferred_element_type=F32)


def nt(a, b):
    return lax.dot_general(a, b, (((1,), (1,)), ((), ())), preferred_element_type=F32)


def one_hot(row, count):
    ids = lax.broadcasted_iota(jnp.int32, (count, row.shape[1]), 0)
    return jnp.where(ids == row, 1.0, 0.0).astype(BF16)


def adagrad(table, acc, grad):
    grown = acc + jnp.sum(grad * grad, axis=0, keepdims=True) * (1.0 / grad.shape[0])
    return table - STEP_SIZE * grad * lax.rsqrt(grown), grown


def bucket(t, spans, idx, ends, tables, outs, work):
    (lidx, ridx, widx, nidx) = idx
    (lhs, rhs, rel) = tables
    (glhs, gctx, grel) = outs
    (left, right, wts, hot_w, qh, ql, qht, qlt, sh, sl, uh, ul, vh, vl, ph, pw, nh, nl) = work
    d, rows = lhs.shape
    rels = rel.shape[1]
    edges = lidx.shape[1]
    neg = nidx.shape[1]
    width = edges // spans
    ats = [pl.ds(c * width, width) for c in range(spans)]
    nats = [pl.ds(c * neg, neg) for c in range(spans)]

    def hot_neg(c):
        return one_hot(nidx[pl.ds(t * spans + c, 1), :], rows)

    rh, rl = split(rhs[...])
    for c in range(spans):
        hot_n = hot_neg(c)
        q = nn(rh, hot_n)
        qh[:, nats[c]] = q.astype(BF16)
        qht[nats[c], :] = q.T.astype(BF16)
        q = nn(rl, hot_n)
        ql[:, nats[c]] = q.astype(BF16)
        qlt[nats[c], :] = q.T.astype(BF16)
    for c in range(spans):
        hot = one_hot(ridx[pl.ds(t, 1), ats[c]], rows)
        right[:, ats[c]] = nn(rh, hot) + nn(rl, hot)
    rh, rl = split(lhs[...])
    for c in range(spans):
        hot = one_hot(lidx[pl.ds(t, 1), ats[c]], rows)
        left[:, ats[c]] = nn(rh, hot) + nn(rl, hot)
    rh, rl = split(rel[...])
    pcoefs, lives = [], []
    for c in range(spans):
        hot = one_hot(widx[pl.ds(t, 1), ats[c]], rels)
        hot_w[:, ats[c]] = hot
        weights = nn(rh, hot) + nn(rl, hot)
        wts[:, ats[c]] = weights
        scaled = left[:, ats[c]] * weights
        high, low = split(scaled)
        sh[:, ats[c]] = high
        sl[:, ats[c]] = low
        slot = lax.broadcasted_iota(jnp.int32, (1, width), 1) + c * width
        live = jnp.where(slot < ends[t], 1.0, 0.0)
        positive = jnp.sum(scaled * right[:, ats[c]], axis=0, keepdims=True)
        pcoef = -jax.nn.sigmoid(-positive) * live
        ph[:, ats[c]], pw[:, ats[c]] = split(pcoef * scaled)
        pcoefs.append(pcoef)
        lives.append(live)
    coefs = []
    for c in range(spans):
        scores = nn(qht[nats[c], :], sh[:, ats[c]]) + (
            nn(qht[nats[c], :], sl[:, ats[c]]) + nn(qlt[nats[c], :], sh[:, ats[c]])
        )
        coefs.append(split(jax.nn.sigmoid(scores) * (lives[c] / neg)))
    for c in range(spans):
        ch, cl = coefs[c]
        mixture = nn(qh[:, nats[c]], ch) + (nn(qh[:, nats[c]], cl) + nn(ql[:, nats[c]], ch))
        toward = pcoefs[c] * right[:, ats[c]] + mixture
        uh[:, ats[c]], ul[:, ats[c]] = split(left[:, ats[c]] * toward)
        vh[:, ats[c]], vl[:, ats[c]] = split(wts[:, ats[c]] * toward)
    for c in range(spans):
        ch, cl = coefs[c]
        ngrad = nt(sh[:, ats[c]], ch) + (nt(sh[:, ats[c]], cl) + nt(sl[:, ats[c]], ch))
        nh[:, nats[c]], nl[:, nats[c]] = split(ngrad)
    total = nt(uh[...], hot_w[...]) + nt(ul[...], hot_w[...])
    for b in range(rels // LANES):
        grel[pl.ds(b * d, d), :] = total[:, b * LANES:(b + 1) * LANES]
    hot = one_hot(lidx[pl.ds(t, 1), :], rows)
    glhs[...] = nt(vh[...], hot) + nt(vl[...], hot)
    hot = one_hot(ridx[pl.ds(t, 1), :], rows)
    total = nt(ph[...], hot) + nt(pw[...], hot)
    hot = jnp.concatenate([hot_neg(c) for c in range(spans)], axis=1)
    gctx[pl.ds(0, d), :] = total + (nt(nh[...], hot) + nt(nl[...], hot))


def work_shapes(d, edges, negs, rels):
    f32 = [pltpu.VMEM((d, edges), F32)] * 3
    bf = lambda *shape: pltpu.VMEM(shape, BF16)
    return f32 + [bf(rels, edges)] + [bf(d, negs)] * 2 + [bf(negs, d)] * 2 + [bf(d, edges)] * 8 + [
        bf(d, negs)
    ] * 2


def halves(core, grel_ref, keep_ref, send_ref, used):
    half = keep_ref.shape[0]
    grel_ref[pl.ds(used, grel_ref.shape[0] - used), :] = jnp.zeros(
        (grel_ref.shape[0] - used, LANES), F32
    )
    keep_ref[...] = grel_ref[pl.ds(pl.multiple_of(core * half, half), half), :]
    send_ref[...] = grel_ref[pl.ds(pl.multiple_of((1 - core) * half, half), half), :]


def first_kernel(spans, core, lidx_hbm, ridx_hbm, nidx_hbm, widx_hbm, ends_hbm, rhs_hbm, lhs_hbm,
                 rel_hbm, racc_hbm, glhs, gctx, keep, send, grel,
                 lidx, ridx, nidx, widx, ends, rhs, lhs, rel, racc, sems, *work):
    sources = (lidx_hbm, ridx_hbm, nidx_hbm, widx_hbm, ends_hbm, rhs_hbm, lhs_hbm, rel_hbm, racc_hbm)
    targets = (lidx, ridx, nidx, widx, ends, rhs, lhs, rel, racc)
    copies = [
        pltpu.make_async_copy(source, target, sems.at[i])
        for i, (source, target) in enumerate(zip(sources, targets))
    ]
    for copy in copies:
        copy.start()
    for copy in copies:
        copy.wait()
    bucket(0, spans, (lidx, ridx, widx, nidx), ends, (lhs, rhs, rel), (glhs, gctx, grel), work)
    tail = gctx.shape[0] - lhs.shape[0]
    gctx[pl.ds(lhs.shape[0], tail), :] = jnp.broadcast_to(racc[...], (tail, racc.shape[1]))
    halves(core[0], grel, keep, send, rel.shape[0] * (rel.shape[1] // LANES))


def join(core, mine, other, grel):
    half = mine.shape[0]
    grel[pl.ds(pl.multiple_of(core * half, half), half), :] = mine[...]
    grel[pl.ds(pl.multiple_of((1 - core) * half, half), half), :] = other[...]


def update_rel(rel, racc, grel, rel_new, racc_new):
    d = rel.shape[0]
    for b in range(rel.shape[1] // LANES):
        at = pl.ds(b * LANES, LANES)
        g = grel[pl.ds(b * d, d), :]
        rel_new[:, at], racc_new[:, at] = adagrad(rel[:, at], racc[:, at], g)


def update_pair(table, acc, one, two, table_new, acc_new):
    table_new[...], acc_new[...] = adagrad(table[...], acc[...], one[...] + two[...])


def second_kernel(spans, lidx, ridx, widx, nidx, ends, core, lhs, rhs, rel, wacc,
                  gw_mine, gw_other, glhs, gctx, keep, send, rel_out, wacc_new,
                  grel, rel_new, sem, *work):
    join(core[0], gw_mine, gw_other, grel)
    update_rel(rel, wacc, grel, rel_new, wacc_new)
    copy = pltpu.make_async_copy(rel_new, rel_out, sem)
    copy.start()
    bucket(1, spans, (lidx, ridx, widx, nidx), ends, (lhs, rhs, rel_new), (glhs, gctx, grel), work)
    halves(core[0], grel, keep, send, rel.shape[0] * (rel.shape[1] // LANES))
    copy.wait()


def moved_kernel(lhs, rhs, lacc, gl_a, gl_b, gc_a, gc_b, lhs_new, rhs_new, lacc_new, racc_new):
    d = lhs.shape[0]
    update_pair(lhs, lacc, gl_a, gl_b, lhs_new, lacc_new)
    update_pair(
        rhs, gc_a.at[pl.ds(d, 1)], gc_a.at[pl.ds(0, d)], gc_b.at[pl.ds(0, d)], rhs_new, racc_new
    )


def pair_kernel(lhs, rhs, lacc, racc, gl_a, gl_b, gc_a, gc_b, lhs_new, rhs_new, lacc_new, racc_new):
    update_pair(lhs, lacc, gl_a, gl_b, lhs_new, lacc_new)
    update_pair(rhs, racc, gc_a, gc_b, rhs_new, racc_new)


def rel_kernel(core, rel, wacc, gw_mine, gw_other, rel_new, wacc_new, grel):
    join(core[0], gw_mine, gw_other, grel)
    update_rel(rel, wacc, grel, rel_new, wacc_new)


def add_kernel(one, two, out):
    out[...] = one[...] + two[...]


def spread_kernel(one, two, *rest):
    out = rest[-1]
    out[...] = jnp.broadcast_to((one[...] + two[...])[None], out.shape)


def follow(value, others):
    return pl.pallas_call(
        lambda *refs: None,
        out_shape=jax.ShapeDtypeStruct(value.shape, value.dtype),
        in_specs=[AN] * (1 + len(others)),
        out_specs=AN,
        input_output_aliases={0: 0},
        compiler_params=pltpu.CompilerParams(vmem_limit_bytes=1 << 20),
    )(value, *others)


VM = pl.BlockSpec(memory_space=pltpu.VMEM)
SM = pl.BlockSpec(memory_space=pltpu.SMEM)
HB = pl.BlockSpec(memory_space=pltpu.HBM)
AN = pl.BlockSpec(memory_space=pl.ANY)


def call(kernel, ins, specs, outs, scratch, flops, mib=4, out_specs={}):
    return pl.pallas_call(
        kernel,
        out_shape=[jax.ShapeDtypeStruct(o, F32) if isinstance(o, tuple) else o for o in outs],
        in_specs=[specs.get(i, VM) for i in range(len(ins))],
        out_specs=[out_specs.get(i, VM) for i in range(len(outs))],
        scratch_shapes=[pltpu.VMEM(s, F32) if isinstance(s, tuple) else s for s in scratch],
        compiler_params=pltpu.CompilerParams(vmem_limit_bytes=mib << 20),
        cost_estimate=pl.CostEstimate(
            flops=flops, bytes_accessed=8_000_000, transcendentals=0
        ),
    )(*ins)


def place(y, x, z, core):
    return y * 32 + x * 16 + z * 2 + core


def near_groups():
    groups = []
    for core in range(2):
        for x in range(2):
            for zh in range(4):
                members = [None] * 8
                for y in range(4):
                    for zl in range(2):
                        z = zh * 2 + zl
                        members[y * 2 + ((z ^ (z >> 1)) & 1)] = place(y, x, z, core)
                groups.append(members)
    return groups


def pairs(move):
    out = []
    for y in range(4):
        for x in range(2):
            for z in range(8):
                for core in range(2):
                    a = place(y, x, z, core)
                    out.append((a, place(*move(y, x, z, core))))
    return out


CORE_PAIRS = pairs(lambda y, x, z, c: (y, x, z, 1 - c))
FAR_PAIRS = (
    pairs(lambda y, x, z, c: (y, x, (z + (1 if z % 2 else 7)) % 8, c)),
    pairs(lambda y, x, z, c: (y, x, z ^ (3 if z in (0, 3, 4, 7) else 7), c)),
    pairs(lambda y, x, z, c: (y, 1 - x, z, c)),
)


def sum_over_blk(keep, send, exchange, after, wait_for):
    got = lax.ppermute(send, "blk", CORE_PAIRS)
    half = keep.shape
    (part,) = call(add_kernel, (keep, got), {}, [half], [], 1_000_000)
    beside = exchange()
    groups = near_groups()
    n = len(groups[0])
    rows = half[0] // n
    got = lax.all_to_all(
        part.reshape(n, rows, LANES), "blk", 0, 0, axis_index_groups=groups
    )
    total = jnp.sum(got, axis=0)
    for move in FAR_PAIRS[:-1]:
        total = total + lax.ppermute(total, "blk", move)
    got = lax.ppermute(total, "blk", FAR_PAIRS[-1])
    ended = tuple(beside[1:])
    (spread,) = call(
        spread_kernel, (total, got) + ended, {2 + i: AN for i in range(len(ended))},
        [(n, rows, LANES)], [], 1_000_000,
    )
    mine = lax.all_to_all(spread, "blk", 0, 0, axis_index_groups=groups)
    beside = after(beside)
    mine = mine.reshape(n * rows, LANES)
    if wait_for:
        mine = follow(mine, tuple(beside[:1]))
    return mine, lax.ppermute(mine, "blk", CORE_PAIRS), beside


def swap(x):
    return lax.ppermute(x, "rel", [(0, 1), (1, 0)])


def onward(x, flip):
    n = lax.axis_size("blk")
    moves = [
        (2 * b + k, 2 * ((b + 1) % n) + (1 - k if flip else k)) for b in range(n) for k in range(2)
    ]
    return lax.ppermute(x, ("blk", "rel"), moves)


def per_device(lhs, rhs, rel, lacc, racc, wacc, lidx, ridx, widx, ends, nidx):
    d, rows = lhs.shape
    rels = rel.shape[1]
    rounds, edges = lidx.shape[2:]
    spans, neg = nidx.shape[3:]
    lidx, ridx, widx = (a.reshape(rounds, edges) for a in (lidx, ridx, widx))
    nidx = nidx.reshape(rounds * spans, neg)
    ends = ends.reshape(rounds)
    lacc, racc, wacc = (a.reshape(1, -1) for a in (lacc, racc, wacc))
    core = lax.rem(lax.axis_index("blk"), 2).astype(jnp.int32).reshape(1)
    used = d * (rels // LANES)
    full = -(-used // 2048) * 2048
    slab, table, state = (d, rows), (d, rels), (1, rows)
    half = (full // 2, LANES)
    work = work_shapes(d, edges, spans * neg, rels)
    sources = tuple(
        pltpu.with_memory_space_constraint(a, pltpu.HBM)
        for a in (lidx, ridx, nidx, widx, ends, rhs, lhs, rel, racc)
    )
    glhs, gctx, keep, send = call(
        functools.partial(first_kernel, spans), (core,) + sources,
        {0: SM} | {1 + i: HB for i in range(9)},
        [slab, (d + 8, rows), half, half],
        [(full, LANES)]
        + [pltpu.VMEM(a.shape, a.dtype) for a in (lidx, ridx, nidx, widx)]
        + [pltpu.SMEM(ends.shape, ends.dtype), slab, slab, table, state, pltpu.SemaphoreType.DMA((9,))]
        + work,
        4_000_000_000, 40,
    )

    rhs_in = onward(rhs, False)

    def exchange_first():
        return glhs, swap(glhs), onward(gctx, False), onward(gctx, True), rhs_in

    def update_first(arrived):
        gl_a, gl_b, gc_a, gc_b, rhs_in = arrived
        return call(
            moved_kernel, (lhs, rhs_in, lacc, gl_a, gl_b, gc_a, gc_b), {},
            [slab, slab, state, state], [], 1_000_000, 2,
        )

    gw_mine, gw_other, (lhs1, rhs1, lacc1, racc1) = sum_over_blk(
        keep, send, exchange_first, update_first, True
    )
    glhs1, gctx1, keep, send, rel, wacc = call(
        functools.partial(second_kernel, spans),
        (lidx, ridx, widx, nidx, ends, core, lhs1, rhs1, rel, wacc, gw_mine, gw_other),
        {4: SM, 5: SM},
        [slab, slab, half, half, pltpu.HBM(table, F32), (1, rels)],
        [(full, LANES), table, pltpu.SemaphoreType.DMA] + work, 4_000_000_000, 40, {4: HB},
    )

    def exchange_last():
        return glhs1, swap(glhs1), gctx1, swap(gctx1)

    def update_last(arrived):
        return call(
            pair_kernel, (lhs1, rhs1, lacc1, racc1) + tuple(arrived), {},
            [slab, slab, state, state], [], 1_000_000, 2,
        )

    gw_mine, gw_other, (lhs, rhs, lacc, racc) = sum_over_blk(
        keep, send, exchange_last, update_last, False
    )
    rel, wacc = call(
        rel_kernel, (core, rel, wacc, gw_mine, gw_other), {0: SM}, [table, (1, rels)],
        [(full, LANES)], 1_000_000, 4,
    )
    return lhs, lacc.reshape(-1), rhs, racc.reshape(-1), rel, wacc.reshape(-1)


def solution(mesh):
    in_specs = (
        P(None, "blk"),
        P(None, "blk"),
        P(None, "rel"),
        P("blk"),
        P("blk"),
        P("rel"),
        P("blk", "rel", None, None),
        P("blk", "rel", None, None),
        P("blk", "rel", None, None),
        P("blk", "rel", None),
        P("blk", "rel", None, None, None),
    )
    out_specs = (P(None, "blk"), P("blk"), P(None, "blk"), P("blk"), P(None, "rel"), P("rel"))
    return jax.shard_map(
        per_device, mesh=mesh, in_specs=in_specs, out_specs=out_specs, check_vma=False
    )
```

```python
import functools

import jax
import jax.numpy as jnp
from jax import lax
from jax.experimental import pallas as pl
from jax.experimental.pallas import tpu as pltpu
from jax.sharding import PartitionSpec as P

STEP_SIZE = 0.2
F32 = jnp.float32
BF16 = jnp.bfloat16
LANES = 128


def split(x):
    hi = x.astype(BF16)
    return hi, (x - hi.astype(F32)).astype(BF16)


def nn(a, b):
    return jnp.dot(a, b, preferred_element_type=F32)


def nt(a, b):
    return lax.dot_general(a, b, (((1,), (1,)), ((), ())), preferred_element_type=F32)


def one_hot(row, count):
    ids = lax.broadcasted_iota(jnp.int32, (count, row.shape[1]), 0)
    return jnp.where(ids == row, 1.0, 0.0).astype(BF16)


def adagrad(table, acc, grad):
    grown = acc + jnp.sum(grad * grad, axis=0, keepdims=True) * (1.0 / grad.shape[0])
    return table - STEP_SIZE * grad * lax.rsqrt(grown), grown


def bucket(t, spans, idx, ends, tables, outs, work):
    (lidx, ridx, widx, nidx) = idx
    (lhs, rhs, rel) = tables
    (glhs, gctx, grel) = outs
    (left, right, wts, hot_w, qh, ql, qht, qlt, sh, sl, uh, ul, vh, vl, ph, pw, nh, nl) = work
    d, rows = lhs.shape
    rels = rel.shape[1]
    edges = lidx.shape[1]
    neg = nidx.shape[1]
    width = edges // spans
    ats = [pl.ds(c * width, width) for c in range(spans)]
    nats = [pl.ds(c * neg, neg) for c in range(spans)]

    def hot_neg(c):
        return one_hot(nidx[pl.ds(t * spans + c, 1), :], rows)

    rh, rl = split(rhs[...])
    for c in range(spans):
        hot_n = hot_neg(c)
        q = nn(rh, hot_n)
        qh[:, nats[c]] = q.astype(BF16)
        qht[nats[c], :] = q.T.astype(BF16)
        q = nn(rl, hot_n)
        ql[:, nats[c]] = q.astype(BF16)
        qlt[nats[c], :] = q.T.astype(BF16)
    for c in range(spans):
        hot = one_hot(ridx[pl.ds(t, 1), ats[c]], rows)
        right[:, ats[c]] = nn(rh, hot) + nn(rl, hot)
    rh, rl = split(lhs[...])
    for c in range(spans):
        hot = one_hot(lidx[pl.ds(t, 1), ats[c]], rows)
        left[:, ats[c]] = nn(rh, hot) + nn(rl, hot)
    rh, rl = split(rel[...])
    pcoefs, lives = [], []
    for c in range(spans):
        hot = one_hot(widx[pl.ds(t, 1), ats[c]], rels)
        hot_w[:, ats[c]] = hot
        weights = nn(rh, hot) + nn(rl, hot)
        wts[:, ats[c]] = weights
        scaled = left[:, ats[c]] * weights
        high, low = split(scaled)
        sh[:, ats[c]] = high
        sl[:, ats[c]] = low
        slot = lax.broadcasted_iota(jnp.int32, (1, width), 1) + c * width
        live = jnp.where(slot < ends[t], 1.0, 0.0)
        positive = jnp.sum(scaled * right[:, ats[c]], axis=0, keepdims=True)
        pcoef = -jax.nn.sigmoid(-positive) * live
        ph[:, ats[c]], pw[:, ats[c]] = split(pcoef * scaled)
        pcoefs.append(pcoef)
        lives.append(live)
    coefs = []
    for c in range(spans):
        scores = nn(qht[nats[c], :], sh[:, ats[c]]) + (
            nn(qht[nats[c], :], sl[:, ats[c]]) + nn(qlt[nats[c], :], sh[:, ats[c]])
        )
        coefs.append(split(jax.nn.sigmoid(scores) * (lives[c] / neg)))
    for c in range(spans):
        ch, cl = coefs[c]
        mixture = nn(qh[:, nats[c]], ch) + (nn(qh[:, nats[c]], cl) + nn(ql[:, nats[c]], ch))
        toward = pcoefs[c] * right[:, ats[c]] + mixture
        uh[:, ats[c]], ul[:, ats[c]] = split(left[:, ats[c]] * toward)
        vh[:, ats[c]], vl[:, ats[c]] = split(wts[:, ats[c]] * toward)
    for c in range(spans):
        ch, cl = coefs[c]
        ngrad = nt(sh[:, ats[c]], ch) + (nt(sh[:, ats[c]], cl) + nt(sl[:, ats[c]], ch))
        nh[:, nats[c]], nl[:, nats[c]] = split(ngrad)
    total = nt(uh[...], hot_w[...]) + nt(ul[...], hot_w[...])
    for b in range(rels // LANES):
        grel[pl.ds(b * d, d), :] = total[:, b * LANES:(b + 1) * LANES]
    hot = one_hot(lidx[pl.ds(t, 1), :], rows)
    glhs[...] = nt(vh[...], hot) + nt(vl[...], hot)
    hot = one_hot(ridx[pl.ds(t, 1), :], rows)
    total = nt(ph[...], hot) + nt(pw[...], hot)
    hot = jnp.concatenate([hot_neg(c) for c in range(spans)], axis=1)
    gctx[pl.ds(0, d), :] = total + (nt(nh[...], hot) + nt(nl[...], hot))


def work_shapes(d, edges, negs, rels):
    f32 = [pltpu.VMEM((d, edges), F32)] * 3
    bf = lambda *shape: pltpu.VMEM(shape, BF16)
    return f32 + [bf(rels, edges)] + [bf(d, negs)] * 2 + [bf(negs, d)] * 2 + [bf(d, edges)] * 8 + [
        bf(d, negs)
    ] * 2


def halves(core, grel_ref, keep_ref, send_ref, used):
    half = keep_ref.shape[0]
    grel_ref[pl.ds(used, grel_ref.shape[0] - used), :] = jnp.zeros(
        (grel_ref.shape[0] - used, LANES), F32
    )
    keep_ref[...] = grel_ref[pl.ds(pl.multiple_of(core * half, half), half), :]
    send_ref[...] = grel_ref[pl.ds(pl.multiple_of((1 - core) * half, half), half), :]


def first_kernel(spans, core, lidx_hbm, ridx_hbm, nidx_hbm, widx_hbm, ends_hbm, rhs_hbm, lhs_hbm,
                 rel_hbm, racc_hbm, glhs, gctx, keep, send, grel,
                 lidx, ridx, nidx, widx, ends, rhs, lhs, rel, racc, sems, *work):
    sources = (lidx_hbm, ridx_hbm, nidx_hbm, widx_hbm, ends_hbm, rhs_hbm, lhs_hbm, rel_hbm, racc_hbm)
    targets = (lidx, ridx, nidx, widx, ends, rhs, lhs, rel, racc)
    copies = [
        pltpu.make_async_copy(source, target, sems.at[i])
        for i, (source, target) in enumerate(zip(sources, targets))
    ]
    for copy in copies:
        copy.start()
    for copy in copies:
        copy.wait()
    bucket(0, spans, (lidx, ridx, widx, nidx), ends, (lhs, rhs, rel), (glhs, gctx, grel), work)
    tail = gctx.shape[0] - lhs.shape[0]
    gctx[pl.ds(lhs.shape[0], tail), :] = jnp.broadcast_to(racc[...], (tail, racc.shape[1]))
    halves(core[0], grel, keep, send, rel.shape[0] * (rel.shape[1] // LANES))


def join(core, mine, other, grel):
    half = mine.shape[0]
    grel[pl.ds(pl.multiple_of(core * half, half), half), :] = mine[...]
    grel[pl.ds(pl.multiple_of((1 - core) * half, half), half), :] = other[...]


def update_rel(rel, racc, grel, rel_new, racc_new):
    d = rel.shape[0]
    for b in range(rel.shape[1] // LANES):
        at = pl.ds(b * LANES, LANES)
        g = grel[pl.ds(b * d, d), :]
        rel_new[:, at], racc_new[:, at] = adagrad(rel[:, at], racc[:, at], g)


def update_pair(table, acc, one, two, table_new, acc_new):
    table_new[...], acc_new[...] = adagrad(table[...], acc[...], one[...] + two[...])


def second_kernel(spans, lidx, ridx, widx, nidx, ends, core, lhs, rhs, rel, wacc,
                  gw_mine, gw_other, both, keep, send, rel_out, wacc_new,
                  grel, rel_new, sem, *work):
    d = lhs.shape[0]
    glhs, gctx = both.at[pl.ds(0, d)], both.at[pl.ds(d, d)]
    join(core[0], gw_mine, gw_other, grel)
    update_rel(rel, wacc, grel, rel_new, wacc_new)
    copy = pltpu.make_async_copy(rel_new, rel_out, sem)
    copy.start()
    bucket(1, spans, (lidx, ridx, widx, nidx), ends, (lhs, rhs, rel_new), (glhs, gctx, grel), work)
    halves(core[0], grel, keep, send, rel.shape[0] * (rel.shape[1] // LANES))
    copy.wait()


def moved_kernel(lhs, rhs, lacc, gl_a, gl_b, gc_a, gc_b, lhs_new, rhs_new, lacc_new, racc_new):
    d = lhs.shape[0]
    update_pair(lhs, lacc, gl_a, gl_b, lhs_new, lacc_new)
    update_pair(
        rhs, gc_a.at[pl.ds(d, 1)], gc_a.at[pl.ds(0, d)], gc_b.at[pl.ds(0, d)], rhs_new, racc_new
    )


def pair_kernel(lhs, rhs, lacc, racc, one, two, lhs_new, rhs_new, lacc_new, racc_new):
    d = lhs.shape[0]
    first, last = pl.ds(0, d), pl.ds(d, d)
    update_pair(lhs, lacc, one.at[first], two.at[first], lhs_new, lacc_new)
    update_pair(rhs, racc, one.at[last], two.at[last], rhs_new, racc_new)


def rel_kernel(core, rel, wacc, gw_mine, gw_other, rel_new, wacc_new, grel):
    join(core[0], gw_mine, gw_other, grel)
    update_rel(rel, wacc, grel, rel_new, wacc_new)


def add_kernel(one, two, out):
    out[...] = one[...] + two[...]


def spread_kernel(one, two, *rest):
    out = rest[-1]
    out[...] = jnp.broadcast_to((one[...] + two[...])[None], out.shape)


def follow(value, others):
    return pl.pallas_call(
        lambda *refs: None,
        out_shape=jax.ShapeDtypeStruct(value.shape, value.dtype),
        in_specs=[AN] * (1 + len(others)),
        out_specs=AN,
        input_output_aliases={0: 0},
        compiler_params=pltpu.CompilerParams(vmem_limit_bytes=1 << 20),
    )(value, *others)


VM = pl.BlockSpec(memory_space=pltpu.VMEM)
SM = pl.BlockSpec(memory_space=pltpu.SMEM)
HB = pl.BlockSpec(memory_space=pltpu.HBM)
AN = pl.BlockSpec(memory_space=pl.ANY)


def call(kernel, ins, specs, outs, scratch, flops, mib=4, out_specs={}):
    return pl.pallas_call(
        kernel,
        out_shape=[jax.ShapeDtypeStruct(o, F32) if isinstance(o, tuple) else o for o in outs],
        in_specs=[specs.get(i, VM) for i in range(len(ins))],
        out_specs=[out_specs.get(i, VM) for i in range(len(outs))],
        scratch_shapes=[pltpu.VMEM(s, F32) if isinstance(s, tuple) else s for s in scratch],
        compiler_params=pltpu.CompilerParams(vmem_limit_bytes=mib << 20),
        cost_estimate=pl.CostEstimate(
            flops=flops, bytes_accessed=8_000_000, transcendentals=0
        ),
    )(*ins)


def place(y, x, z, core):
    return y * 32 + x * 16 + z * 2 + core


def near_groups():
    groups = []
    for core in range(2):
        for x in range(2):
            for zh in range(4):
                members = [None] * 8
                for y in range(4):
                    for zl in range(2):
                        z = zh * 2 + zl
                        members[y * 2 + ((z ^ (z >> 1)) & 1)] = place(y, x, z, core)
                groups.append(members)
    return groups


def pairs(move):
    out = []
    for y in range(4):
        for x in range(2):
            for z in range(8):
                for core in range(2):
                    a = place(y, x, z, core)
                    out.append((a, place(*move(y, x, z, core))))
    return out


CORE_PAIRS = pairs(lambda y, x, z, c: (y, x, z, 1 - c))
FAR_PAIRS = (
    pairs(lambda y, x, z, c: (y, x, (z + (1 if z % 2 else 7)) % 8, c)),
    pairs(lambda y, x, z, c: (y, x, z ^ (3 if z in (0, 3, 4, 7) else 7), c)),
    pairs(lambda y, x, z, c: (y, 1 - x, z, c)),
)


def sum_over_blk(keep, send, exchange, after, wait_for):
    got = lax.ppermute(send, "blk", CORE_PAIRS)
    half = keep.shape
    (part,) = call(add_kernel, (keep, got), {}, [half], [], 1_000_000)
    beside = exchange()
    groups = near_groups()
    n = len(groups[0])
    rows = half[0] // n
    got = lax.all_to_all(
        part.reshape(n, rows, LANES), "blk", 0, 0, axis_index_groups=groups
    )
    total = jnp.sum(got, axis=0)
    for move in FAR_PAIRS[:-1]:
        total = total + lax.ppermute(total, "blk", move)
    got = lax.ppermute(total, "blk", FAR_PAIRS[-1])
    ended = tuple(beside[1:])
    (spread,) = call(
        spread_kernel, (total, got) + ended, {2 + i: AN for i in range(len(ended))},
        [(n, rows, LANES)], [], 1_000_000,
    )
    mine = lax.all_to_all(spread, "blk", 0, 0, axis_index_groups=groups)
    beside = after(beside)
    mine = mine.reshape(n * rows, LANES)
    if wait_for:
        mine = follow(mine, tuple(beside[:1]))
    return mine, lax.ppermute(mine, "blk", CORE_PAIRS), beside


def swap(x):
    return lax.ppermute(x, "rel", [(0, 1), (1, 0)])


def onward(x, flip):
    n = lax.axis_size("blk")
    moves = [
        (2 * b + k, 2 * ((b + 1) % n) + (1 - k if flip else k)) for b in range(n) for k in range(2)
    ]
    return lax.ppermute(x, ("blk", "rel"), moves)


def per_device(lhs, rhs, rel, lacc, racc, wacc, lidx, ridx, widx, ends, nidx):
    d, rows = lhs.shape
    rels = rel.shape[1]
    rounds, edges = lidx.shape[2:]
    spans, neg = nidx.shape[3:]
    lidx, ridx, widx = (a.reshape(rounds, edges) for a in (lidx, ridx, widx))
    nidx = nidx.reshape(rounds * spans, neg)
    ends = ends.reshape(rounds)
    lacc, racc, wacc = (a.reshape(1, -1) for a in (lacc, racc, wacc))
    core = lax.rem(lax.axis_index("blk"), 2).astype(jnp.int32).reshape(1)
    used = d * (rels // LANES)
    full = -(-used // 2048) * 2048
    slab, table, state = (d, rows), (d, rels), (1, rows)
    half = (full // 2, LANES)
    work = work_shapes(d, edges, spans * neg, rels)
    sources = tuple(
        pltpu.with_memory_space_constraint(a, pltpu.HBM)
        for a in (lidx, ridx, nidx, widx, ends, rhs, lhs, rel, racc)
    )
    glhs, gctx, keep, send = call(
        functools.partial(first_kernel, spans), (core,) + sources,
        {0: SM} | {1 + i: HB for i in range(9)},
        [slab, (d + 8, rows), half, half],
        [(full, LANES)]
        + [pltpu.VMEM(a.shape, a.dtype) for a in (lidx, ridx, nidx, widx)]
        + [pltpu.SMEM(ends.shape, ends.dtype), slab, slab, table, state, pltpu.SemaphoreType.DMA((9,))]
        + work,
        4_000_000_000, 40,
    )

    rhs_in = onward(rhs, False)

    def exchange_first():
        return glhs, swap(glhs), onward(gctx, False), onward(gctx, True), rhs_in

    def update_first(arrived):
        gl_a, gl_b, gc_a, gc_b, rhs_in = arrived
        return call(
            moved_kernel, (lhs, rhs_in, lacc, gl_a, gl_b, gc_a, gc_b), {},
            [slab, slab, state, state], [], 1_000_000, 2,
        )

    gw_mine, gw_other, (lhs1, rhs1, lacc1, racc1) = sum_over_blk(
        keep, send, exchange_first, update_first, True
    )
    grads, keep, send, rel, wacc = call(
        functools.partial(second_kernel, spans),
        (lidx, ridx, widx, nidx, ends, core, lhs1, rhs1, rel, wacc, gw_mine, gw_other),
        {4: SM, 5: SM},
        [(2 * d, rows), half, half, pltpu.HBM(table, F32), (1, rels)],
        [(full, LANES), table, pltpu.SemaphoreType.DMA] + work, 4_000_000_000, 40, {3: HB},
    )

    def exchange_last():
        return grads, swap(grads)

    def update_last(arrived):
        return call(
            pair_kernel, (lhs1, rhs1, lacc1, racc1) + tuple(arrived), {},
            [slab, slab, state, state], [], 1_000_000, 2,
        )

    gw_mine, gw_other, (lhs, rhs, lacc, racc) = sum_over_blk(
        keep, send, exchange_last, update_last, False
    )
    rel, wacc = call(
        rel_kernel, (core, rel, wacc, gw_mine, gw_other), {0: SM}, [table, (1, rels)],
        [(full, LANES)], 1_000_000, 4,
    )
    return lhs, lacc.reshape(-1), rhs, racc.reshape(-1), rel, wacc.reshape(-1)


def solution(mesh):
    in_specs = (
        P(None, "blk"),
        P(None, "blk"),
        P(None, "rel"),
        P("blk"),
        P("blk"),
        P("rel"),
        P("blk", "rel", None, None),
        P("blk", "rel", None, None),
        P("blk", "rel", None, None),
        P("blk", "rel", None),
        P("blk", "rel", None, None, None),
    )
    out_specs = (P(None, "blk"), P("blk"), P(None, "blk"), P("blk"), P(None, "rel"), P("rel"))
    return jax.shard_map(
        per_device, mesh=mesh, in_specs=in_specs, out_specs=out_specs, check_vma=False
    )
```

```python
import functools

import jax
import jax.numpy as jnp
from jax import lax
from jax.experimental import pallas as pl
from jax.experimental.pallas import tpu as pltpu
from jax.sharding import PartitionSpec as P

STEP_SIZE = 0.2
F32 = jnp.float32
BF16 = jnp.bfloat16
LANES = 128


def split(x):
    hi = x.astype(BF16)
    return hi, (x - hi.astype(F32)).astype(BF16)


def nn(a, b):
    return jnp.dot(a, b, preferred_element_type=F32)


def nt(a, b):
    return lax.dot_general(a, b, (((1,), (1,)), ((), ())), preferred_element_type=F32)


def one_hot(row, count):
    ids = lax.broadcasted_iota(jnp.int32, (count, row.shape[1]), 0)
    return jnp.where(ids == row, 1.0, 0.0).astype(BF16)


def adagrad(table, acc, grad):
    grown = acc + jnp.sum(grad * grad, axis=0, keepdims=True) * (1.0 / grad.shape[0])
    return table - STEP_SIZE * grad * lax.rsqrt(grown), grown


def bucket(t, spans, idx, ends, tables, outs, work):
    (lidx, ridx, widx, nidx) = idx
    (lhs, rhs, rel) = tables
    (glhs, gctx, grel) = outs
    (left, right, wts, hot_w, qh, ql, qht, qlt, sh, sl, uh, ul, vh, vl, ph, pw, nh, nl) = work
    d, rows = lhs.shape
    rels = rel.shape[1]
    edges = lidx.shape[1]
    neg = nidx.shape[1]
    width = edges // spans
    ats = [pl.ds(c * width, width) for c in range(spans)]
    nats = [pl.ds(c * neg, neg) for c in range(spans)]

    def hot_neg(c):
        return one_hot(nidx[pl.ds(t * spans + c, 1), :], rows)

    rh, rl = split(rhs[...])
    for c in range(0, spans, 2):
        some = range(c, min(c + 2, spans))
        hot_n = jnp.concatenate([hot_neg(i) for i in some], axis=1)
        at = pl.ds(c * neg, len(some) * neg)
        q = nn(rh, hot_n)
        qh[:, at] = q.astype(BF16)
        qht[at, :] = q.T.astype(BF16)
        q = nn(rl, hot_n)
        ql[:, at] = q.astype(BF16)
        qlt[at, :] = q.T.astype(BF16)
    for c in range(spans):
        hot = one_hot(ridx[pl.ds(t, 1), ats[c]], rows)
        right[:, ats[c]] = nn(rh, hot) + nn(rl, hot)
    rh, rl = split(lhs[...])
    for c in range(spans):
        hot = one_hot(lidx[pl.ds(t, 1), ats[c]], rows)
        left[:, ats[c]] = nn(rh, hot) + nn(rl, hot)
    rh, rl = split(rel[...])
    pcoefs, lives = [], []
    for c in range(spans):
        hot = one_hot(widx[pl.ds(t, 1), ats[c]], rels)
        hot_w[:, ats[c]] = hot
        weights = nn(rh, hot) + nn(rl, hot)
        wts[:, ats[c]] = weights
        scaled = left[:, ats[c]] * weights
        high, low = split(scaled)
        sh[:, ats[c]] = high
        sl[:, ats[c]] = low
        slot = lax.broadcasted_iota(jnp.int32, (1, width), 1) + c * width
        live = jnp.where(slot < ends[t], 1.0, 0.0)
        positive = jnp.sum(scaled * right[:, ats[c]], axis=0, keepdims=True)
        pcoef = -jax.nn.sigmoid(-positive) * live
        ph[:, ats[c]], pw[:, ats[c]] = split(pcoef * scaled)
        pcoefs.append(pcoef)
        lives.append(live)
    coefs = []
    for c in range(spans):
        scores = nn(qht[nats[c], :], sh[:, ats[c]]) + (
            nn(qht[nats[c], :], sl[:, ats[c]]) + nn(qlt[nats[c], :], sh[:, ats[c]])
        )
        coefs.append(split(jax.nn.sigmoid(scores) * (lives[c] / neg)))
    for c in range(spans):
        ch, cl = coefs[c]
        high = qh[:, nats[c]]
        mixture = nn(
            jnp.concatenate([high, high], axis=1), jnp.concatenate([ch, cl], axis=0)
        ) + nn(ql[:, nats[c]], ch)
        toward = pcoefs[c] * right[:, ats[c]] + mixture
        uh[:, ats[c]], ul[:, ats[c]] = split(left[:, ats[c]] * toward)
        vh[:, ats[c]], vl[:, ats[c]] = split(wts[:, ats[c]] * toward)
    for c in range(spans):
        ch, cl = coefs[c]
        ngrad = nt(sh[:, ats[c]], ch) + (nt(sh[:, ats[c]], cl) + nt(sl[:, ats[c]], ch))
        nh[:, nats[c]], nl[:, nats[c]] = split(ngrad)
    total = nt(uh[...], hot_w[...]) + nt(ul[...], hot_w[...])
    for b in range(rels // LANES):
        grel[pl.ds(b * d, d), :] = total[:, b * LANES:(b + 1) * LANES]
    hot = one_hot(lidx[pl.ds(t, 1), :], rows)
    glhs[...] = nt(vh[...], hot) + nt(vl[...], hot)
    hot = one_hot(ridx[pl.ds(t, 1), :], rows)
    total = nt(ph[...], hot) + nt(pw[...], hot)
    hot = jnp.concatenate([hot_neg(c) for c in range(spans)], axis=1)
    gctx[pl.ds(0, d), :] = total + (nt(nh[...], hot) + nt(nl[...], hot))


def work_shapes(d, edges, negs, rels):
    f32 = [pltpu.VMEM((d, edges), F32)] * 3
    bf = lambda *shape: pltpu.VMEM(shape, BF16)
    return f32 + [bf(rels, edges)] + [bf(d, negs)] * 2 + [bf(negs, d)] * 2 + [bf(d, edges)] * 8 + [
        bf(d, negs)
    ] * 2


def halves(core, grel_ref, keep_ref, send_ref, used):
    half = keep_ref.shape[0]
    grel_ref[pl.ds(used, grel_ref.shape[0] - used), :] = jnp.zeros(
        (grel_ref.shape[0] - used, LANES), F32
    )
    keep_ref[...] = grel_ref[pl.ds(pl.multiple_of(core * half, half), half), :]
    send_ref[...] = grel_ref[pl.ds(pl.multiple_of((1 - core) * half, half), half), :]


def first_kernel(spans, core, lidx_hbm, ridx_hbm, nidx_hbm, widx_hbm, ends_hbm, rhs_hbm, lhs_hbm,
                 rel_hbm, racc_hbm, glhs, gctx, keep, send, grel,
                 lidx, ridx, nidx, widx, ends, rhs, lhs, rel, racc, sems, *work):
    sources = (lidx_hbm, ridx_hbm, nidx_hbm, widx_hbm, ends_hbm, rhs_hbm, lhs_hbm, rel_hbm, racc_hbm)
    targets = (lidx, ridx, nidx, widx, ends, rhs, lhs, rel, racc)
    copies = [
        pltpu.make_async_copy(source, target, sems.at[i])
        for i, (source, target) in enumerate(zip(sources, targets))
    ]
    for copy in copies:
        copy.start()
    for copy in copies:
        copy.wait()
    bucket(0, spans, (lidx, ridx, widx, nidx), ends, (lhs, rhs, rel), (glhs, gctx, grel), work)
    tail = gctx.shape[0] - lhs.shape[0]
    gctx[pl.ds(lhs.shape[0], tail), :] = jnp.broadcast_to(racc[...], (tail, racc.shape[1]))
    halves(core[0], grel, keep, send, rel.shape[0] * (rel.shape[1] // LANES))


def join(core, mine, other, grel):
    half = mine.shape[0]
    grel[pl.ds(pl.multiple_of(core * half, half), half), :] = mine[...]
    grel[pl.ds(pl.multiple_of((1 - core) * half, half), half), :] = other[...]


def update_rel(rel, racc, grel, rel_new, racc_new):
    d = rel.shape[0]
    for b in range(rel.shape[1] // LANES):
        at = pl.ds(b * LANES, LANES)
        g = grel[pl.ds(b * d, d), :]
        rel_new[:, at], racc_new[:, at] = adagrad(rel[:, at], racc[:, at], g)


def update_pair(table, acc, one, two, table_new, acc_new):
    table_new[...], acc_new[...] = adagrad(table[...], acc[...], one[...] + two[...])


def second_kernel(spans, lidx, ridx, widx, nidx, ends, core, lhs, rhs, rel, wacc,
                  gw_mine, gw_other, both, keep, send, rel_out, wacc_new,
                  grel, rel_new, sem, *work):
    d = lhs.shape[0]
    glhs, gctx = both.at[pl.ds(0, d)], both.at[pl.ds(d, d)]
    join(core[0], gw_mine, gw_other, grel)
    update_rel(rel, wacc, grel, rel_new, wacc_new)
    copy = pltpu.make_async_copy(rel_new, rel_out, sem)
    copy.start()
    bucket(1, spans, (lidx, ridx, widx, nidx), ends, (lhs, rhs, rel_new), (glhs, gctx, grel), work)
    halves(core[0], grel, keep, send, rel.shape[0] * (rel.shape[1] // LANES))
    copy.wait()


def moved_kernel(lhs, rhs, lacc, gl_a, gl_b, gc_a, gc_b, lhs_new, rhs_new, lacc_new, racc_new):
    d = lhs.shape[0]
    update_pair(lhs, lacc, gl_a, gl_b, lhs_new, lacc_new)
    update_pair(
        rhs, gc_a.at[pl.ds(d, 1)], gc_a.at[pl.ds(0, d)], gc_b.at[pl.ds(0, d)], rhs_new, racc_new
    )


def pair_kernel(lhs, rhs, lacc, racc, one, two, lhs_new, rhs_new, lacc_new, racc_new):
    d = lhs.shape[0]
    first, last = pl.ds(0, d), pl.ds(d, d)
    update_pair(lhs, lacc, one.at[first], two.at[first], lhs_new, lacc_new)
    update_pair(rhs, racc, one.at[last], two.at[last], rhs_new, racc_new)


def rel_kernel(core, rel, wacc, gw_mine, gw_other, rel_new, wacc_new, grel):
    join(core[0], gw_mine, gw_other, grel)
    update_rel(rel, wacc, grel, rel_new, wacc_new)


def add_kernel(one, two, out):
    out[...] = one[...] + two[...]


def spread_kernel(one, two, *rest):
    out = rest[-1]
    out[...] = jnp.broadcast_to((one[...] + two[...])[None], out.shape)


def follow(value, others):
    return pl.pallas_call(
        lambda *refs: None,
        out_shape=jax.ShapeDtypeStruct(value.shape, value.dtype),
        in_specs=[AN] * (1 + len(others)),
        out_specs=AN,
        input_output_aliases={0: 0},
        compiler_params=pltpu.CompilerParams(vmem_limit_bytes=1 << 20),
    )(value, *others)


VM = pl.BlockSpec(memory_space=pltpu.VMEM)
SM = pl.BlockSpec(memory_space=pltpu.SMEM)
HB = pl.BlockSpec(memory_space=pltpu.HBM)
AN = pl.BlockSpec(memory_space=pl.ANY)


def call(kernel, ins, specs, outs, scratch, flops, mib=4, out_specs={}):
    return pl.pallas_call(
        kernel,
        out_shape=[jax.ShapeDtypeStruct(o, F32) if isinstance(o, tuple) else o for o in outs],
        in_specs=[specs.get(i, VM) for i in range(len(ins))],
        out_specs=[out_specs.get(i, VM) for i in range(len(outs))],
        scratch_shapes=[pltpu.VMEM(s, F32) if isinstance(s, tuple) else s for s in scratch],
        compiler_params=pltpu.CompilerParams(vmem_limit_bytes=mib << 20),
        cost_estimate=pl.CostEstimate(
            flops=flops, bytes_accessed=8_000_000, transcendentals=0
        ),
    )(*ins)


def place(y, x, z, core):
    return y * 32 + x * 16 + z * 2 + core


def near_groups():
    groups = []
    for core in range(2):
        for x in range(2):
            for zh in range(4):
                members = [None] * 8
                for y in range(4):
                    for zl in range(2):
                        z = zh * 2 + zl
                        members[y * 2 + ((z ^ (z >> 1)) & 1)] = place(y, x, z, core)
                groups.append(members)
    return groups


def pairs(move):
    out = []
    for y in range(4):
        for x in range(2):
            for z in range(8):
                for core in range(2):
                    a = place(y, x, z, core)
                    out.append((a, place(*move(y, x, z, core))))
    return out


CORE_PAIRS = pairs(lambda y, x, z, c: (y, x, z, 1 - c))
FAR_PAIRS = (
    pairs(lambda y, x, z, c: (y, x, (z + (1 if z % 2 else 7)) % 8, c)),
    pairs(lambda y, x, z, c: (y, x, z ^ (3 if z in (0, 3, 4, 7) else 7), c)),
    pairs(lambda y, x, z, c: (y, 1 - x, z, c)),
)


def sum_over_blk(keep, send, exchange, after, wait_for):
    got = lax.ppermute(send, "blk", CORE_PAIRS)
    half = keep.shape
    (part,) = call(add_kernel, (keep, got), {}, [half], [], 1_000_000)
    beside = exchange()
    groups = near_groups()
    n = len(groups[0])
    rows = half[0] // n
    got = lax.all_to_all(
        part.reshape(n, rows, LANES), "blk", 0, 0, axis_index_groups=groups
    )
    total = jnp.sum(got, axis=0)
    for move in FAR_PAIRS[:-1]:
        total = total + lax.ppermute(total, "blk", move)
    got = lax.ppermute(total, "blk", FAR_PAIRS[-1])
    ended = tuple(beside[1:])
    (spread,) = call(
        spread_kernel, (total, got) + ended, {2 + i: AN for i in range(len(ended))},
        [(n, rows, LANES)], [], 1_000_000,
    )
    mine = lax.all_to_all(spread, "blk", 0, 0, axis_index_groups=groups)
    beside = after(beside)
    mine = mine.reshape(n * rows, LANES)
    if wait_for:
        mine = follow(mine, tuple(beside[:1]))
    return mine, lax.ppermute(mine, "blk", CORE_PAIRS), beside


def swap(x):
    return lax.ppermute(x, "rel", [(0, 1), (1, 0)])


def onward(x, flip):
    n = lax.axis_size("blk")
    moves = [
        (2 * b + k, 2 * ((b + 1) % n) + (1 - k if flip else k)) for b in range(n) for k in range(2)
    ]
    return lax.ppermute(x, ("blk", "rel"), moves)


def per_device(lhs, rhs, rel, lacc, racc, wacc, lidx, ridx, widx, ends, nidx):
    d, rows = lhs.shape
    rels = rel.shape[1]
    rounds, edges = lidx.shape[2:]
    spans, neg = nidx.shape[3:]
    lidx, ridx, widx = (a.reshape(rounds, edges) for a in (lidx, ridx, widx))
    nidx = nidx.reshape(rounds * spans, neg)
    ends = ends.reshape(rounds)
    lacc, racc, wacc = (a.reshape(1, -1) for a in (lacc, racc, wacc))
    core = lax.rem(lax.axis_index("blk"), 2).astype(jnp.int32).reshape(1)
    used = d * (rels // LANES)
    full = -(-used // 2048) * 2048
    slab, table, state = (d, rows), (d, rels), (1, rows)
    half = (full // 2, LANES)
    work = work_shapes(d, edges, spans * neg, rels)
    sources = tuple(
        pltpu.with_memory_space_constraint(a, pltpu.HBM)
        for a in (lidx, ridx, nidx, widx, ends, rhs, lhs, rel, racc)
    )
    glhs, gctx, keep, send = call(
        functools.partial(first_kernel, spans), (core,) + sources,
        {0: SM} | {1 + i: HB for i in range(9)},
        [slab, (d + 8, rows), half, half],
        [(full, LANES)]
        + [pltpu.VMEM(a.shape, a.dtype) for a in (lidx, ridx, nidx, widx)]
        + [pltpu.SMEM(ends.shape, ends.dtype), slab, slab, table, state, pltpu.SemaphoreType.DMA((9,))]
        + work,
        4_000_000_000, 40,
    )

    rhs_in = onward(rhs, False)

    def exchange_first():
        return glhs, swap(glhs), onward(gctx, False), onward(gctx, True), rhs_in

    def update_first(arrived):
        gl_a, gl_b, gc_a, gc_b, rhs_in = arrived
        return call(
            moved_kernel, (lhs, rhs_in, lacc, gl_a, gl_b, gc_a, gc_b), {},
            [slab, slab, state, state], [], 1_000_000, 2,
        )

    gw_mine, gw_other, (lhs1, rhs1, lacc1, racc1) = sum_over_blk(
        keep, send, exchange_first, update_first, True
    )
    grads, keep, send, rel, wacc = call(
        functools.partial(second_kernel, spans),
        (lidx, ridx, widx, nidx, ends, core, lhs1, rhs1, rel, wacc, gw_mine, gw_other),
        {4: SM, 5: SM},
        [(2 * d, rows), half, half, pltpu.HBM(table, F32), (1, rels)],
        [(full, LANES), table, pltpu.SemaphoreType.DMA] + work, 4_000_000_000, 40, {3: HB},
    )

    def exchange_last():
        return grads, swap(grads)

    def update_last(arrived):
        return call(
            pair_kernel, (lhs1, rhs1, lacc1, racc1) + tuple(arrived), {},
            [slab, slab, state, state], [], 1_000_000, 2,
        )

    gw_mine, gw_other, (lhs, rhs, lacc, racc) = sum_over_blk(
        keep, send, exchange_last, update_last, False
    )
    rel, wacc = call(
        rel_kernel, (core, rel, wacc, gw_mine, gw_other), {0: SM}, [table, (1, rels)],
        [(full, LANES)], 1_000_000, 4,
    )
    return lhs, lacc.reshape(-1), rhs, racc.reshape(-1), rel, wacc.reshape(-1)


def solution(mesh):
    in_specs = (
        P(None, "blk"),
        P(None, "blk"),
        P(None, "rel"),
        P("blk"),
        P("blk"),
        P("rel"),
        P("blk", "rel", None, None),
        P("blk", "rel", None, None),
        P("blk", "rel", None, None),
        P("blk", "rel", None),
        P("blk", "rel", None, None, None),
    )
    out_specs = (P(None, "blk"), P("blk"), P(None, "blk"), P("blk"), P(None, "rel"), P("rel"))
    return jax.shard_map(
        per_device, mesh=mesh, in_specs=in_specs, out_specs=out_specs, check_vma=False
    )
```
